512 devices in a mesh: pp: 16 (over y, x), ep: 32 (over z, core).
Axes of the slice: x: 4, y: 4, z: 16, core: 2. Of those that a mesh axis runs over, the one named last changes fastest.
Arguments:
- upstream: bfloat16 [16, 4096, 3584], P('pp', 'ep'), may hold values from -0.375 to 0.375
- routes: int32 [16, 4096, 2], P('pp', 'ep'), may hold values from 0 to 3, all different within a row; in each aligned block of 128 rows (0 to 127, 128 to 255, ..., all dimensions but the last counted through in order) at most 120 rows name the same one
- gates: float32 [16, 4096, 2], P('pp', 'ep'), may hold values from 0.1 to 1.2
- hidden_saved: bfloat16 [16, 32, 960, 512], P('pp', 'ep'), may hold values from -6 to 6
- down_weight: bfloat16 [16, 32, 512, 896], P('pp', 'ep'), as said below
- first_moment: bfloat16 [16, 32, 256, 896], P('pp', 'ep'), may hold values from -1.796875 to 1.796875
- second_moment: bfloat16 [16, 32, 256, 896], P('pp', 'ep'), may hold values from 0.25 to 4
Outputs:
- gate_grad: float32 [16, 4096, 2], P('pp', 'ep')
- new_weight: bfloat16 [16, 32, 256, 896], P('pp', 'ep')
- new_first: bfloat16 [16, 32, 256, 896], P('pp', 'ep')
- new_second: bfloat16 [16, 32, 256, 896], P('pp', 'ep')
The draws below stay inside these ranges and needn't reach their ends.
Inputs may be any that keep to these rules, and one draw needn't show every extreme that they name: `routes`: each row names 2 different experts. Within the rows of one device no expert is named more than 120 times, a bound that some block reaches. down_weight[i] equals down_weight[15 - i]: a rank and its mirror hold the same section.
All inputs are finite; a program needn't handle non-finite values.
Results may differ from the reference program's by a relative error of at most 0.005.
Values may be sent and summed in bfloat16 or wider, within the bound.
No kernel may reach another device: no remote copies, remote signals or barrier semaphores. Data moves between devices by JAX's collectives and lax.ppermute only.
A program may use at most 128 MiB of HBM per device.

```python
import math
import jax
import jax.numpy as jnp
import numpy as np
from jax import lax

DW = 3584
FW = 1024
EXP = 4
TOP = 2
SPLITS = 2
TOK_DEV = 128
CAP = 120
FEAT = 4
F_DEV = 512
D_DEV = 896
HALF_F = 256
TOKENS = 4096
ROWS = 3840
N_PP = 16
N_EP = 32


def draw_down_weight(key, part):
    key = jax.random.fold_in(key, 7)
    sections = jax.random.normal(key, (N_PP // 2, N_EP, F_DEV, D_DEV), jnp.float32) * FW ** (-0.5)
    return jnp.concatenate([sections, sections[::-1]], axis=0).astype(jnp.bfloat16)


def steps_of(rng, dims, cuts, least, largest):
    gain = 1.0
    for axis_at, blocks in cuts:
        steps = jax.random.uniform(jax.random.fold_in(jax.random.fold_in(rng, 6), axis_at), (blocks,), jnp.float32, least / len(cuts), largest / len(cuts))
        gain = gain * jnp.repeat(jnp.exp(steps), dims[axis_at] // blocks).reshape((-1,) + (1,) * (len(dims) - 1 - axis_at))
    return gain


def routed_block(key, own, number, rows, count, top, reach, slope):
    sequence = jax.random.permutation(key, count)
    packed, usual = load_shares(count, rows * top, reach, slope, True), load_shares(count, rows * top, reach, slope, False)
    places = jnp.arange(count)

    def named(lengths, offset_by):
        used = int((lengths > 0).sum())
        fixed = max(1, used // 4)
        passed = fixed + (places - fixed + offset_by * (used - fixed)) % max(1, count - fixed)
        return jnp.zeros((count,), jnp.int32).at[sequence[jnp.where(places < fixed, places, passed)]].set(jnp.asarray(lengths, jnp.int32))

    lengths = jnp.where(number % 4 == 0, named(packed, number // 4), named(usual, number - number // 4 - 1))
    mixed = jax.random.permutation(jax.random.fold_in(own, 3), count)
    donor, receiver = mixed[0:count // 2 * 2:2], mixed[1:count // 2 * 2:2]
    room = jnp.minimum(lengths[donor] - 1, reach - lengths[receiver]) // 2
    room = jnp.where((donor == sequence[0]) | (receiver == sequence[0]) | (lengths[receiver] == 0), 0, jnp.maximum(room, 0))
    passed = jax.random.randint(jax.random.fold_in(own, 4), (count // 2,), 0, 1 << 20) % (room + 1)
    lengths = lengths.at[donor].add(-passed).at[receiver].add(passed)
    labels = jnp.searchsorted(jnp.cumsum(lengths), jnp.arange(rows * top), side="right").astype(jnp.int32)
    listing = labels.reshape(top, rows).T
    listing = listing[jax.random.permutation(jax.random.fold_in(own, 1), rows)]
    offset_by = jax.random.randint(jax.random.fold_in(own, 2), (rows, 1), 0, top)
    return jnp.take_along_axis(listing, (jnp.arange(top)[None, :] + offset_by) % top, axis=1)


def load_shares(count, total, bound, lean, full):
    loads = [(1 << 20) // math.isqrt(grade ** lean) + 1 for grade in range(1, count + 1)]
    largest = bound if full else min(bound, max(-(-total // count), total * loads[0] // sum(loads)))
    least = 1 if total - largest >= count - 1 else 0
    given, surplus = [largest] + [least] * (count - 1), total - largest - least * (count - 1)
    while surplus > 0:
        movable = [i for i in range(1, count) if given[i] < largest] or [i for i in range(1, count) if given[i] < bound]
        whole, left = sum([loads[i] for i in movable]), surplus
        for i in movable:
            more = min(bound - given[i], max(1, left * loads[i] // whole), surplus)
            given[i] = given[i] + more
            surplus = surplus - more
    return np.array(given)


def gaussian(rng, shape, width, reach, pieces=(), kind=jnp.bfloat16):
    result = width * jax.random.normal(rng, shape, jnp.float32)
    if pieces:
        result = result * steps_of(rng, shape, pieces, -0.22, 0.18)
    return jnp.clip(result, -reach, reach).astype(kind)


def setup_inputs(seed: int = 0) -> dict:
    arg_keys = jax.random.split(jax.random.key(seed), 8)
    upstream = gaussian(arg_keys[0], (N_PP, TOKENS, DW), 0.0625, 0.375, ((0, 16), (1, 32)))
    routes_keys = jax.random.split(jax.random.fold_in(arg_keys[1], 1), N_PP * TOKENS // TOK_DEV)
    routes_turns = jax.random.permutation(jax.random.fold_in(arg_keys[1], 3), N_PP * TOKENS // TOK_DEV)
    routes = jax.vmap(lambda own, number: routed_block(jax.random.fold_in(arg_keys[1], 2), own, number, TOK_DEV, EXP, TOP, CAP, 2))(routes_keys, routes_turns).reshape((N_PP, TOKENS, TOP))
    gates = jnp.clip(0.1 + 1.1 * jax.random.uniform(arg_keys[2], (N_PP, TOKENS, TOP), jnp.float32) ** steps_of(arg_keys[2], (N_PP, TOKENS, TOP), ((0, 16), (1, 32)), -0.2, 0.2), 0.1, 1.2)
    hidden_saved = gaussian(arg_keys[3], (N_PP, N_EP, ROWS // FEAT, F_DEV), 1.0, 6.0, ((0, 16), (1, 32)))
    down_weight = draw_down_weight(jax.random.fold_in(arg_keys[7], 71), 0)
    first_moment = gaussian(arg_keys[5], (N_PP, N_EP, HALF_F, D_DEV), 0.3, 1.796875, ((0, 16), (1, 32)))
    second_moment = jnp.clip(jnp.exp(math.log(4.0) - 2.7725887 * jax.random.uniform(arg_keys[6], (N_PP, N_EP, HALF_F, D_DEV), jnp.float32) ** steps_of(arg_keys[6], (N_PP, N_EP, HALF_F, D_DEV), ((0, 16), (1, 32)), -0.2, 0.2)), 0.25, 4.0).astype(jnp.bfloat16)
    return {"upstream": upstream, "routes": routes, "gates": gates, "hidden_saved": hidden_saved, "down_weight": down_weight, "first_moment": first_moment, "second_moment": second_moment}


beta_first = 0.9
beta_second = 0.95
learn_rate = 0.00022
decay_rate = 0.1
epsilon = 1e-08
step_count = 10

def slot_numbers(route_rows):
    flat_routes = route_rows.reshape(-1)
    onehot = (flat_routes[:, None] == jnp.arange(EXP, dtype=jnp.int32)[None, :]).astype(jnp.int32)
    before = jnp.cumsum(onehot, axis=0) - onehot
    return lax.optimization_barrier(jnp.sum(before * onehot, axis=1)).astype(jnp.int32)

def place_rows(upstream_dev, routes_dev, gates_dev):
    scaled = (gates_dev[:, :, None] * upstream_dev[:, None, :].astype(jnp.float32)).astype(jnp.bfloat16)
    slot_table = slot_numbers(routes_dev).reshape(routes_dev.shape)
    buffer = jnp.zeros((EXP, CAP, DW), jnp.bfloat16).at[routes_dev, slot_table].set(scaled)
    return (buffer, slot_table)

def lookup(table_dev, routes_dev, slots_dev, gates_dev):
    return table_dev[routes_dev, slots_dev] / gates_dev

def rank_terms(inputs):
    upstream_rank, routes_rank, gates_rank, hidden_rank, weight_rank = inputs
    routes_dev = routes_rank.reshape(N_EP, TOK_DEV, TOP)
    gates_dev = gates_rank.reshape(N_EP, TOK_DEV, TOP)
    buffers, slot_table = jax.vmap(place_rows)(upstream_rank.reshape(N_EP, TOK_DEV, DW), routes_dev, gates_dev)
    hidden_blocks = hidden_rank.reshape(EXP, SPLITS, FEAT, ROWS // FEAT, F_DEV)
    weight_blocks = weight_rank.reshape(EXP, SPLITS, FEAT, F_DEV, D_DEV)
    grad_list = []
    dot_list = []
    for expert in range(EXP):
        expert_rows = buffers[:, expert].reshape(ROWS, DW)
        hidden = hidden_blocks[expert].transpose(1, 2, 0, 3).reshape(ROWS, FW)
        weight = weight_blocks[expert].transpose(0, 2, 1, 3).reshape(FW, DW)
        grad_list.append(lax.dot_general(hidden, expert_rows, (((0,), (0,)), ((), ())), preferred_element_type=jnp.float32))
        output = jnp.dot(hidden, weight, preferred_element_type=jnp.float32)
        dot_list.append(lax.optimization_barrier(jnp.sum(expert_rows.astype(jnp.float32) * output, axis=1)).reshape(N_EP, CAP))
    grad_blocks = jnp.stack(grad_list).reshape(EXP, SPLITS, F_DEV, FEAT, D_DEV).transpose(0, 1, 3, 2, 4)
    grad_blocks = grad_blocks.reshape(N_EP, F_DEV, D_DEV).astype(jnp.bfloat16)
    dot_table = jnp.stack(dot_list, axis=1)
    gate_grad = jax.vmap(lookup)(dot_table, routes_dev, slot_table, gates_dev).reshape(TOKENS, TOP)
    return (grad_blocks, gate_grad)

def reference(upstream, routes, gates, hidden_saved, down_weight, first_moment, second_moment):
    grad_blocks, gate_grad = lax.map(rank_terms, (upstream, routes, gates, hidden_saved, down_weight))
    mirrored = grad_blocks[::-1]
    pair_total = grad_blocks.astype(jnp.float32) + mirrored.astype(jnp.float32)
    lower_rank = (jnp.arange(N_PP) < N_PP // 2)[:, None, None, None]
    kept_grad = jnp.where(lower_rank, pair_total[:, :, :HALF_F], pair_total[:, :, HALF_F:])
    weight_kept = jnp.where(lower_rank, down_weight[:, :, :HALF_F], down_weight[:, :, HALF_F:]).astype(jnp.float32)
    first_new = beta_first * first_moment.astype(jnp.float32) + (1.0 - beta_first) * kept_grad
    second_new = beta_second * second_moment.astype(jnp.float32) + (1.0 - beta_second) * kept_grad * kept_grad
    first_hat = first_new / (1.0 - beta_first ** step_count)
    second_hat = second_new / (1.0 - beta_second ** step_count)
    new_weight = weight_kept - learn_rate * (first_hat / (jnp.sqrt(second_hat) + epsilon) + decay_rate * weight_kept)
    return (gate_grad, new_weight.astype(jnp.bfloat16), first_new.astype(jnp.bfloat16), second_new.astype(jnp.bfloat16))
```

```python
import jax
import jax.numpy as jnp
from jax import lax
from jax.experimental import pallas as pl
from jax.experimental.pallas import tpu as pltpu
from jax.sharding import PartitionSpec as P

EXP = 4
TOP = 2
SPLITS = 2
CAP = 120

beta_first = 0.9
beta_second = 0.95
learn_rate = 0.00022
decay_rate = 0.1
epsilon = 1e-08
step_count = 10

VMEM_BYTES = 40 * 1024 * 1024

OFFSETS = (0, -1, 1, -2, 2, -3, 3, -4, 4, -5, 5, -6, 6, -7, 7, 8)
ROUNDS = ((0, 5), (5, 9), (9, 13), (13, 16))


def send_chips(block, hops):
    count = lax.axis_size("ep")
    return lax.ppermute(block, "ep", [(i, (i + 2 * hops) % count) for i in range(count)])


def swap_bits(block, bits):
    count = lax.axis_size("ep")
    return lax.ppermute(block, "ep", [(i, i ^ bits) for i in range(count)])


def place_kernel(index, meta, rows, out):
    expert, core = index[16], index[17]
    tokens = meta.shape[2]
    lower = lax.broadcasted_iota(jnp.int32, (tokens, tokens), 0) > lax.broadcasted_iota(
        jnp.int32, (tokens, tokens), 1
    )
    lower = lower.astype(jnp.float32).astype(jnp.bfloat16)
    slots = rows.shape[0]
    lane = lax.broadcasted_iota(jnp.int32, (tokens, slots), 1).astype(jnp.float32)
    wanted = expert.astype(jnp.float32)
    for half in range(2):
        owner = core if half == 0 else 1 - core
        table = jnp.transpose(meta[owner])
        first = table[:, 0:1] == wanted
        second = table[:, 1:2] == wanted
        named = jnp.where(first | second, 1.0, 0.0)
        gate = jnp.where(first, table[:, 2:3], 0.0) + jnp.where(second, table[:, 3:4], 0.0)
        wide = jnp.broadcast_to(named, (tokens, slots))
        before = jnp.dot(lower, wide.astype(jnp.bfloat16), preferred_element_type=jnp.float32)
        place = before + (owner * CAP).astype(jnp.float32)
        onehot = jnp.where(place == lane, wide, 0.0).astype(jnp.bfloat16)
        picked = jnp.dot(onehot, rows[...], preferred_element_type=jnp.float32)
        out[0, half * tokens : (half + 1) * tokens, :] = (gate * picked).astype(out.dtype)


def place_rows(index, meta, hidden):
    tokens = meta.shape[2]
    units = hidden.shape[1]
    return pl.pallas_call(
        place_kernel,
        grid_spec=pltpu.PrefetchScalarGridSpec(
            num_scalar_prefetch=1,
            grid=(16,),
            in_specs=[
                pl.BlockSpec((2, 8, tokens), lambda i, ix: (ix[i], 0, 0)),
                pl.BlockSpec((2 * CAP, units), lambda i, ix: (ix[18 + i], 0)),
            ],
            out_specs=pl.BlockSpec((1, 2 * tokens, units), lambda i, ix: (i, 0, 0)),
        ),
        out_shape=jax.ShapeDtypeStruct((16, 2 * tokens, units), jnp.bfloat16),
        cost_estimate=pl.CostEstimate(
            flops=2 * 16 * 256 * 240 * (units + 128), bytes_accessed=16 * 512 * units * 2, transcendentals=0
        ),
        compiler_params=pltpu.CompilerParams(vmem_limit_bytes=VMEM_BYTES),
        name="place_rows",
    )(index, meta, hidden)


def block_dots(index, start, rows, hidden, weight, dots):
    for b, part in enumerate(rows):
        output = jnp.dot(hidden[b], weight[...], preferred_element_type=jnp.float32)
        column = jnp.sum(part[...].astype(jnp.float32) * output, axis=1, keepdims=True)
        line = jnp.transpose(jnp.broadcast_to(column, (column.shape[0], 128)))[0:1]
        for half in range(2):
            owner = index[34 + 2 * (start + b) + half]
            dots[pl.ds(owner, 1)] = line[:, half * 128 : (half + 1) * 128].reshape(1, 1, 128)


def add_grads(rows, hidden, before, after):
    total = None if before is None else before[...]
    for b, part in enumerate(rows):
        term = lax.dot_general(
            hidden[b], part[...], (((0,), (0,)), ((), ())), preferred_element_type=jnp.float32
        )
        total = term if total is None else total + term
    after[...] = total.astype(after.dtype)


def round_call(index, start, rows, placed, weight, grads, dots):
    count = len(rows)
    units, width = weight.shape
    tokens = rows[0].shape[0]
    first = grads is None

    def kernel(ix, hid, wgt, *refs):
        parts, refs = refs[:count], refs[count:]
        if first:
            grads_out, dots_out = refs
            dots_out[...] = jnp.zeros_like(dots_out)
            grads_in = None
        else:
            grads_in, dots_in, grads_out, dots_out = refs
            dots_out[...] = dots_in[...]
        block_dots(ix, start, parts, hid, wgt, dots_out)
        add_grads(parts, hid, grads_in, grads_out)

    whole = lambda shape: pl.BlockSpec(shape, lambda i, ix: (0,) * len(shape))
    hid_spec = pl.BlockSpec((count, tokens, units), lambda i, ix: (0, 0, 0))
    in_specs = [hid_spec, whole(weight.shape)] + [whole(rows[0].shape)] * count
    operands = [placed, weight, *rows]
    aliases = {}
    if not first:
        in_specs += [whole((units, width)), whole((32, 1, 128))]
        operands += [grads, dots]
        aliases = {count + 3: 0, count + 4: 1}
    return pl.pallas_call(
        kernel,
        grid_spec=pltpu.PrefetchScalarGridSpec(
            num_scalar_prefetch=1,
            grid=(1,),
            in_specs=in_specs,
            out_specs=[whole((units, width)), whole((32, 1, 128))],
        ),
        out_shape=[
            jax.ShapeDtypeStruct((units, width), jnp.float32),
            jax.ShapeDtypeStruct((32, 1, 128), jnp.float32),
        ],
        input_output_aliases=aliases,
        cost_estimate=pl.CostEstimate(
            flops=4 * count * tokens * units * width,
            bytes_accessed=8 * units * width + count * tokens * (units + width) * 2,
            transcendentals=0,
        ),
        compiler_params=pltpu.CompilerParams(vmem_limit_bytes=VMEM_BYTES),
        name="round_blocks",
    )(index, *operands)


def last_dots(index, start, rows, placed, weight, dots):
    count = len(rows)
    tokens = rows[0].shape[0]

    def kernel(ix, hid, wgt, *refs):
        parts, (dots_in, dots_out) = refs[:count], refs[count:]
        dots_out[...] = dots_in[...]
        block_dots(ix, start, parts, hid, wgt, dots_out)

    whole = lambda shape: pl.BlockSpec(shape, lambda i, ix: (0,) * len(shape))
    return pl.pallas_call(
        kernel,
        grid_spec=pltpu.PrefetchScalarGridSpec(
            num_scalar_prefetch=1,
            grid=(1,),
            in_specs=[whole(placed.shape), whole(weight.shape)]
            + [whole(rows[0].shape)] * count
            + [whole((32, 1, 128))],
            out_specs=whole((32, 1, 128)),
        ),
        out_shape=jax.ShapeDtypeStruct((32, 1, 128), jnp.float32),
        input_output_aliases={count + 3: 0},
        cost_estimate=pl.CostEstimate(
            flops=2 * count * tokens * weight.size, bytes_accessed=2 * weight.size, transcendentals=0
        ),
        compiler_params=pltpu.CompilerParams(vmem_limit_bytes=VMEM_BYTES),
        name="last_dots",
    )(index, *([placed, weight, *rows, dots]))


def last_grads(which, rows, placed, grads):
    count = len(rows)
    tokens = rows[0].shape[0]
    units, width = grads.shape
    half = units // 2

    def kernel(ix, hid, grads_in, *refs):
        parts, (out,) = refs[:count], refs[count:]
        add_grads(parts, hid, grads_in, out)

    whole = lambda shape: pl.BlockSpec(shape, lambda i, ix: (0,) * len(shape))
    return pl.pallas_call(
        kernel,
        grid_spec=pltpu.PrefetchScalarGridSpec(
            num_scalar_prefetch=1,
            grid=(1,),
            in_specs=[
                pl.BlockSpec((count, tokens, half), lambda i, ix: (0, 0, ix[0])),
                pl.BlockSpec((half, width), lambda i, ix: (ix[0], 0)),
            ]
            + [whole(rows[0].shape)] * count,
            out_specs=whole((half, width)),
        ),
        out_shape=jax.ShapeDtypeStruct((half, width), jnp.bfloat16),
        cost_estimate=pl.CostEstimate(
            flops=2 * count * tokens * half * width, bytes_accessed=6 * half * width, transcendentals=0
        ),
        compiler_params=pltpu.CompilerParams(vmem_limit_bytes=VMEM_BYTES),
        name="last_grads",
    )(which, placed, grads, *rows)


def shards(upstream, routes, gates, hidden_saved, down_weight, first_moment, second_moment):
    rows_in = upstream[0]
    route_dev = routes[0]
    gate_dev = gates[0]
    weight = down_weight[0, 0]
    tokens, row_width = rows_in.shape
    units, part = weight.shape
    position = lax.axis_index("ep")
    chip, core = position // 2, position % 2
    parity = chip % 2
    expert, block = position // 8, position % 4

    source = (chip + jnp.array(OFFSETS, jnp.int32)) % 16
    hidden_at = ((source // 4) ^ block) * 4 + source % 4
    owners = (2 * source[:, None] + (core ^ jnp.arange(2, dtype=jnp.int32))[None, :]).reshape(-1)
    index = jnp.concatenate([source, jnp.stack([expert, core]), hidden_at, owners]).astype(jnp.int32)

    def features(at):
        return lax.dynamic_slice(rows_in, (0, at * part), (tokens, part))

    outgoing = jnp.stack([features(block ^ 1), features(block ^ 3)])
    incoming = swap_bits(outgoing, 1)
    same = jnp.concatenate([features(block), incoming[0]], axis=0)
    diff = jnp.concatenate([features(block ^ 2), incoming[1]], axis=0)

    own_hidden = hidden_saved[0, 0]
    chip_hidden = swap_bits(own_hidden, 2)
    meta = jnp.concatenate([route_dev.astype(jnp.float32), gate_dev], axis=1)
    meta = jnp.pad(meta.T, ((0, 4), (0, 0)))
    meta = jnp.broadcast_to(meta[None], (lax.axis_size("ep"),) + meta.shape)

    diff_steps = [(send_chips(diff, 1), send_chips(diff, -1))]
    same_steps = [(send_chips(same, 2), send_chips(same, -2))]
    grads = dots = placed = None
    for step in range(1, 4):
        ahead = diff_steps[-1] if step == 1 else diff_steps[-1] + same_steps[-2]
        if step == 3:
            ahead = ahead + (placed,)
        ahead = lax.optimization_barrier(ahead)
        diff_steps.append((send_chips(ahead[0], 2), send_chips(ahead[1], -2)))
        ahead = same_steps[-1] + diff_steps[-2]
        if step == 3:
            ahead = ahead + (grads,)
        ahead = lax.optimization_barrier(ahead)
        if step == 1:
            meta = lax.optimization_barrier((meta,) + ahead[:2])[0]
            meta = lax.all_to_all(meta, "ep", split_axis=0, concat_axis=0, tiled=True)
            hidden = jnp.concatenate(
                [own_hidden, swap_bits(own_hidden, 1), chip_hidden, swap_bits(chip_hidden, 1)],
                axis=0,
            )
            placed = place_rows(index, meta, hidden)
        if step < 3:
            same_steps.append((send_chips(ahead[0], 2), send_chips(ahead[1], -2)))
        else:
            across = jnp.concatenate(
                [send_chips(ahead[0][:tokens], 2), send_chips(ahead[1][tokens:], -2)], axis=0
            )
        if step > 1:
            start, stop = ROUNDS[step - 2]
            rows = list(diff_steps[step - 2] + same_steps[step - 2])
            rows = [same] + rows if step == 2 else rows
            grads, dots = round_call(index, start, rows, placed[start:stop], weight, grads, dots)
    start, stop = ROUNDS[2]
    rows = list(diff_steps[2] + same_steps[2])
    grads, dots = round_call(index, start, rows, placed[start:stop], weight, grads, dots)
    far_forth, far_back = diff_steps[3]
    last = [far_forth, far_back, across]
    start, stop = ROUNDS[3]
    placed_last = placed[start:stop]

    pipe_rank = lax.axis_index("pp")
    rank_count = lax.axis_size("pp")
    upper = (pipe_rank >= rank_count // 2).astype(jnp.int32)
    half_units = units // 2
    moving = last_grads(jnp.stack([1 - upper]), last, placed_last, grads)
    moving = lax.ppermute(moving, "pp", [(i, rank_count - 1 - i) for i in range(rank_count)])
    dots = last_dots(index, start, last, placed_last, weight, dots)
    returned = lax.all_to_all(dots, "ep", split_axis=0, concat_axis=0, tiled=True)
    kept = last_grads(jnp.stack([upper]), last, placed_last, grads)

    summed = kept.astype(jnp.float32) + moving.astype(jnp.float32)
    weight_kept = lax.dynamic_slice(weight, (upper * half_units, 0), (half_units, part)).astype(
        jnp.float32
    )
    first_new = beta_first * first_moment[0, 0].astype(jnp.float32) + (1.0 - beta_first) * summed
    second_new = (
        beta_second * second_moment[0, 0].astype(jnp.float32)
        + (1.0 - beta_second) * summed * summed
    )
    first_hat = first_new / (1.0 - beta_first**step_count)
    second_hat = second_new / (1.0 - beta_second**step_count)
    new_weight = weight_kept - learn_rate * (
        first_hat / (jnp.sqrt(second_hat) + epsilon) + decay_rate * weight_kept
    )

    totals = jnp.sum(returned.reshape(EXP, 8, tokens), axis=1)
    named = route_dev[:, :, None] == jnp.arange(EXP, dtype=jnp.int32)[None, None, :]
    gate_grad = jnp.sum(jnp.where(named, totals.T[:, None, :], 0.0), axis=2) / gate_dev
    return (
        gate_grad[None],
        new_weight.astype(jnp.bfloat16)[None, None],
        first_new.astype(jnp.bfloat16)[None, None],
        second_new.astype(jnp.bfloat16)[None, None],
    )


def solution(mesh):
    placed = (
        P("pp", "ep", None),
        P("pp", "ep", None),
        P("pp", "ep", None),
        P("pp", "ep", None, None),
        P("pp", "ep", None, None),
        P("pp", "ep", None, None),
        P("pp", "ep", None, None),
    )
    return jax.shard_map(
        shards,
        mesh=mesh,
        in_specs=placed,
        out_specs=(
            P("pp", "ep", None),
            P("pp", "ep", None, None),
            P("pp", "ep", None, None),
            P("pp", "ep", None, None),
        ),
        check_vma=False,
    )
```

```python
import jax
import jax.numpy as jnp
from jax import lax
from jax.experimental import pallas as pl
from jax.experimental.pallas import tpu as pltpu
from jax.sharding import PartitionSpec as P

EXP = 4
TOP = 2
SPLITS = 2
CAP = 120

beta_first = 0.9
beta_second = 0.95
learn_rate = 0.00022
decay_rate = 0.1
epsilon = 1e-08
step_count = 10

VMEM_BYTES = 40 * 1024 * 1024

OFFSETS = (0, -1, 1, -2, 2, -3, 3, -4, 4, -5, 5, -6, 6, -7, 7, 8)
ROUNDS = ((0, 5), (5, 9), (9, 13), (13, 16))


def send_chips(block, hops):
    count = lax.axis_size("ep")
    return lax.ppermute(block, "ep", [(i, (i + 2 * hops) % count) for i in range(count)])


def swap_bits(block, bits):
    count = lax.axis_size("ep")
    return lax.ppermute(block, "ep", [(i, i ^ bits) for i in range(count)])


def place_kernel(index, meta, rows, out):
    expert, core = index[16], index[17]
    tokens = meta.shape[2]
    lower = lax.broadcasted_iota(jnp.int32, (tokens, tokens), 0) > lax.broadcasted_iota(
        jnp.int32, (tokens, tokens), 1
    )
    lower = lower.astype(jnp.float32).astype(jnp.bfloat16)
    slots = rows.shape[0]
    lane = lax.broadcasted_iota(jnp.int32, (tokens, slots), 1).astype(jnp.float32)
    wanted = expert.astype(jnp.float32)
    for half in range(2):
        owner = core if half == 0 else 1 - core
        table = jnp.transpose(meta[owner])
        first = table[:, 0:1] == wanted
        second = table[:, 1:2] == wanted
        named = jnp.where(first | second, 1.0, 0.0)
        gate = jnp.where(first, table[:, 2:3], 0.0) + jnp.where(second, table[:, 3:4], 0.0)
        wide = jnp.broadcast_to(named, (tokens, slots))
        before = jnp.dot(lower, wide.astype(jnp.bfloat16), preferred_element_type=jnp.float32)
        place = before + (owner * CAP).astype(jnp.float32)
        onehot = jnp.where(place == lane, wide, 0.0).astype(jnp.bfloat16)
        picked = jnp.dot(onehot, rows[...], preferred_element_type=jnp.float32)
        out[0, half * tokens : (half + 1) * tokens, :] = (gate * picked).astype(out.dtype)


def place_rows(index, meta, hidden, start, stop):
    tokens = meta.shape[2]
    units = hidden.shape[1]
    count = stop - start
    return pl.pallas_call(
        place_kernel,
        grid_spec=pltpu.PrefetchScalarGridSpec(
            num_scalar_prefetch=1,
            grid=(count,),
            in_specs=[
                pl.BlockSpec((2, 8, tokens), lambda i, ix: (ix[start + i], 0, 0)),
                pl.BlockSpec((2 * CAP, units), lambda i, ix: (ix[18 + start + i], 0)),
            ],
            out_specs=pl.BlockSpec((1, 2 * tokens, units), lambda i, ix: (i, 0, 0)),
        ),
        out_shape=jax.ShapeDtypeStruct((count, 2 * tokens, units), jnp.bfloat16),
        cost_estimate=pl.CostEstimate(
            flops=2 * count * 256 * 240 * (units + 128), bytes_accessed=count * 512 * units * 2, transcendentals=0
        ),
        compiler_params=pltpu.CompilerParams(vmem_limit_bytes=VMEM_BYTES),
        name="place_rows",
    )(index, meta, hidden)


def block_dots(index, start, rows, hidden, weight, dots):
    for b, part in enumerate(rows):
        output = jnp.dot(hidden[b], weight[...], preferred_element_type=jnp.float32)
        column = jnp.sum(part[...].astype(jnp.float32) * output, axis=1, keepdims=True)
        line = jnp.transpose(jnp.broadcast_to(column, (column.shape[0], 128)))[0:1]
        for half in range(2):
            owner = index[34 + 2 * (start + b) + half]
            dots[pl.ds(owner, 1)] = line[:, half * 128 : (half + 1) * 128].reshape(1, 1, 128)


def add_grads(rows, hidden, before, after):
    total = None if before is None else before[...]
    for b, part in enumerate(rows):
        term = lax.dot_general(
            hidden[b], part[...], (((0,), (0,)), ((), ())), preferred_element_type=jnp.float32
        )
        total = term if total is None else total + term
    after[...] = total.astype(after.dtype)


def round_call(index, start, rows, placed, weight, grads, dots):
    count = len(rows)
    units, width = weight.shape
    tokens = rows[0].shape[0]
    first = grads is None

    def kernel(ix, hid, wgt, *refs):
        parts, refs = refs[:count], refs[count:]
        if first:
            grads_out, dots_out = refs
            dots_out[...] = jnp.zeros_like(dots_out)
            grads_in = None
        else:
            grads_in, dots_in, grads_out, dots_out = refs
            dots_out[...] = dots_in[...]
        block_dots(ix, start, parts, hid, wgt, dots_out)
        add_grads(parts, hid, grads_in, grads_out)

    whole = lambda shape: pl.BlockSpec(shape, lambda i, ix: (0,) * len(shape))
    hid_spec = pl.BlockSpec((count, tokens, units), lambda i, ix: (0, 0, 0))
    in_specs = [hid_spec, whole(weight.shape)] + [whole(rows[0].shape)] * count
    operands = [placed, weight, *rows]
    aliases = {}
    if not first:
        in_specs += [whole((units, width)), whole((32, 1, 128))]
        operands += [grads, dots]
        aliases = {count + 3: 0, count + 4: 1}
    return pl.pallas_call(
        kernel,
        grid_spec=pltpu.PrefetchScalarGridSpec(
            num_scalar_prefetch=1,
            grid=(1,),
            in_specs=in_specs,
            out_specs=[whole((units, width)), whole((32, 1, 128))],
        ),
        out_shape=[
            jax.ShapeDtypeStruct((units, width), jnp.float32),
            jax.ShapeDtypeStruct((32, 1, 128), jnp.float32),
        ],
        input_output_aliases=aliases,
        cost_estimate=pl.CostEstimate(
            flops=4 * count * tokens * units * width,
            bytes_accessed=8 * units * width + count * tokens * (units + width) * 2,
            transcendentals=0,
        ),
        compiler_params=pltpu.CompilerParams(vmem_limit_bytes=VMEM_BYTES),
        name="round_blocks",
    )(index, *operands)


def last_dots(index, start, rows, placed, weight, dots):
    count = len(rows)
    tokens = rows[0].shape[0]

    def kernel(ix, hid, wgt, *refs):
        parts, (dots_in, dots_out) = refs[:count], refs[count:]
        dots_out[...] = dots_in[...]
        block_dots(ix, start, parts, hid, wgt, dots_out)

    whole = lambda shape: pl.BlockSpec(shape, lambda i, ix: (0,) * len(shape))
    return pl.pallas_call(
        kernel,
        grid_spec=pltpu.PrefetchScalarGridSpec(
            num_scalar_prefetch=1,
            grid=(1,),
            in_specs=[whole(placed.shape), whole(weight.shape)]
            + [whole(rows[0].shape)] * count
            + [whole((32, 1, 128))],
            out_specs=whole((32, 1, 128)),
        ),
        out_shape=jax.ShapeDtypeStruct((32, 1, 128), jnp.float32),
        input_output_aliases={count + 3: 0},
        cost_estimate=pl.CostEstimate(
            flops=2 * count * tokens * weight.size, bytes_accessed=2 * weight.size, transcendentals=0
        ),
        compiler_params=pltpu.CompilerParams(vmem_limit_bytes=VMEM_BYTES),
        name="last_dots",
    )(index, *([placed, weight, *rows, dots]))


def last_grads(which, rows, placed, grads):
    count = len(rows)
    tokens = rows[0].shape[0]
    units, width = grads.shape
    half = units // 2

    def kernel(ix, hid, grads_in, *refs):
        parts, (out,) = refs[:count], refs[count:]
        add_grads(parts, hid, grads_in, out)

    whole = lambda shape: pl.BlockSpec(shape, lambda i, ix: (0,) * len(shape))
    return pl.pallas_call(
        kernel,
        grid_spec=pltpu.PrefetchScalarGridSpec(
            num_scalar_prefetch=1,
            grid=(1,),
            in_specs=[
                pl.BlockSpec((count, tokens, half), lambda i, ix: (0, 0, ix[0])),
                pl.BlockSpec((half, width), lambda i, ix: (ix[0], 0)),
            ]
            + [whole(rows[0].shape)] * count,
            out_specs=whole((half, width)),
        ),
        out_shape=jax.ShapeDtypeStruct((half, width), jnp.bfloat16),
        cost_estimate=pl.CostEstimate(
            flops=2 * count * tokens * half * width, bytes_accessed=6 * half * width, transcendentals=0
        ),
        compiler_params=pltpu.CompilerParams(vmem_limit_bytes=VMEM_BYTES),
        name="last_grads",
    )(which, placed, grads, *rows)


def shards(upstream, routes, gates, hidden_saved, down_weight, first_moment, second_moment):
    rows_in = upstream[0]
    route_dev = routes[0]
    gate_dev = gates[0]
    weight = down_weight[0, 0]
    tokens, row_width = rows_in.shape
    units, part = weight.shape
    position = lax.axis_index("ep")
    chip, core = position // 2, position % 2
    parity = chip % 2
    expert, block = position // 8, position % 4

    source = (chip + jnp.array(OFFSETS, jnp.int32)) % 16
    hidden_at = ((source // 4) ^ block) * 4 + source % 4
    owners = (2 * source[:, None] + (core ^ jnp.arange(2, dtype=jnp.int32))[None, :]).reshape(-1)
    index = jnp.concatenate([source, jnp.stack([expert, core]), hidden_at, owners]).astype(jnp.int32)

    def features(at):
        return lax.dynamic_slice(rows_in, (0, at * part), (tokens, part))

    tie = lax.optimization_barrier
    own_hidden = hidden_saved[0, 0]
    chip_hidden = swap_bits(own_hidden, 2)
    outgoing = jnp.stack([features(block ^ 1), features(block ^ 3)])
    incoming = swap_bits(outgoing, 1)
    core_hidden = swap_bits(own_hidden, 1)
    same = jnp.concatenate([features(block), incoming[0]], axis=0)
    diff = jnp.concatenate([features(block ^ 2), incoming[1]], axis=0)
    meta = jnp.concatenate([route_dev.astype(jnp.float32), gate_dev], axis=1)
    meta = jnp.pad(meta.T, ((0, 4), (0, 0)))
    meta = jnp.broadcast_to(meta[None], (lax.axis_size("ep"),) + meta.shape)
    meta = lax.all_to_all(meta, "ep", split_axis=0, concat_axis=0, tiled=True)
    same, diff, chip_hidden, core_hidden = tie((same, diff, chip_hidden, core_hidden))

    def step(pair, hops, *done):
        pair = tie((*pair, *done)) if done else pair
        return send_chips(pair[0], hops), send_chips(pair[1], -hops)

    def round_at(number, rows, grads, dots):
        start, stop = ROUNDS[number]
        placed = place_rows(index, meta, hidden, start, stop)
        return round_call(index, start, rows, placed, weight, grads, dots)

    d1 = step((diff, diff), 1)
    s1 = step((same, same), 2)
    far_hidden = swap_bits(chip_hidden, 1)
    hidden = jnp.concatenate([own_hidden, core_hidden, chip_hidden, far_hidden], axis=0)
    d2 = step(d1, 2)
    s2 = step(s1, 2, meta)
    d3 = step(d2, 2)
    s3 = step(s2, 2)
    grads, dots = round_at(0, [same, *d1, *s1], None, None)
    d4 = step(d3, 2)
    grads1, dots = round_at(1, [*d2, *s2], grads, dots)
    ahead = tie((*s3,))
    across = (send_chips(ahead[0][:tokens], 2), send_chips(ahead[1][tokens:], -2))
    grads, dots = round_at(2, [*d3, *s3], grads1, dots)
    start, stop = ROUNDS[3]
    last = [*d4, jnp.concatenate(across, axis=0)]
    placed_last = place_rows(index, meta, hidden, start, stop)

    pipe_rank = lax.axis_index("pp")
    rank_count = lax.axis_size("pp")
    upper = (pipe_rank >= rank_count // 2).astype(jnp.int32)
    half_units = units // 2
    moving = last_grads(jnp.stack([1 - upper]), last, placed_last, grads)
    moving = lax.ppermute(moving, "pp", [(i, rank_count - 1 - i) for i in range(rank_count)])
    dots = last_dots(index, start, last, placed_last, weight, dots)
    returned = lax.all_to_all(dots, "ep", split_axis=0, concat_axis=0, tiled=True)
    kept = last_grads(jnp.stack([upper]), last, placed_last, grads)

    summed = kept.astype(jnp.float32) + moving.astype(jnp.float32)
    weight_kept = lax.dynamic_slice(weight, (upper * half_units, 0), (half_units, part)).astype(
        jnp.float32
    )
    first_new = beta_first * first_moment[0, 0].astype(jnp.float32) + (1.0 - beta_first) * summed
    second_new = (
        beta_second * second_moment[0, 0].astype(jnp.float32)
        + (1.0 - beta_second) * summed * summed
    )
    first_hat = first_new / (1.0 - beta_first**step_count)
    second_hat = second_new / (1.0 - beta_second**step_count)
    new_weight = weight_kept - learn_rate * (
        first_hat / (jnp.sqrt(second_hat) + epsilon) + decay_rate * weight_kept
    )

    totals = jnp.sum(returned.reshape(EXP, 8, tokens), axis=1)
    named = route_dev[:, :, None] == jnp.arange(EXP, dtype=jnp.int32)[None, None, :]
    gate_grad = jnp.sum(jnp.where(named, totals.T[:, None, :], 0.0), axis=2) / gate_dev
    return (
        gate_grad[None],
        new_weight.astype(jnp.bfloat16)[None, None],
        first_new.astype(jnp.bfloat16)[None, None],
        second_new.astype(jnp.bfloat16)[None, None],
    )


def solution(mesh):
    placed = (
        P("pp", "ep", None),
        P("pp", "ep", None),
        P("pp", "ep", None),
        P("pp", "ep", None, None),
        P("pp", "ep", None, None),
        P("pp", "ep", None, None),
        P("pp", "ep", None, None),
    )
    return jax.shard_map(
        shards,
        mesh=mesh,
        in_specs=placed,
        out_specs=(
            P("pp", "ep", None),
            P("pp", "ep", None, None),
            P("pp", "ep", None, None),
            P("pp", "ep", None, None),
        ),
        check_vma=False,
    )
```

```python
import jax
import jax.numpy as jnp
from jax import lax
from jax.experimental import pallas as pl
from jax.experimental.pallas import tpu as pltpu
from jax.sharding import PartitionSpec as P

EXP = 4
TOP = 2
SPLITS = 2
CAP = 120

beta_first = 0.9
beta_second = 0.95
learn_rate = 0.00022
decay_rate = 0.1
epsilon = 1e-08
step_count = 10

VMEM_BYTES = 40 * 1024 * 1024

OFFSETS = (0, -1, 1, -2, 2, -3, 3, -4, 4, -5, 5, -6, 6, -7, 7, 8)
ROUNDS = ((0, 5), (5, 9), (9, 13), (13, 16))


def send_chips(block, hops):
    count = lax.axis_size("ep")
    return lax.ppermute(block, "ep", [(i, (i + 2 * hops) % count) for i in range(count)])


def swap_bits(block, bits):
    count = lax.axis_size("ep")
    return lax.ppermute(block, "ep", [(i, i ^ bits) for i in range(count)])


def place_kernel(index, meta, rows, out):
    expert, core = index[16], index[17]
    tokens = meta.shape[2]
    lower = lax.broadcasted_iota(jnp.int32, (tokens, tokens), 0) > lax.broadcasted_iota(
        jnp.int32, (tokens, tokens), 1
    )
    lower = lower.astype(jnp.float32).astype(jnp.bfloat16)
    slots = rows.shape[0]
    lane = lax.broadcasted_iota(jnp.int32, (tokens, slots), 1).astype(jnp.float32)
    wanted = expert.astype(jnp.float32)
    for half in range(2):
        owner = core if half == 0 else 1 - core
        table = jnp.transpose(meta[owner])
        first = table[:, 0:1] == wanted
        second = table[:, 1:2] == wanted
        named = jnp.where(first | second, 1.0, 0.0)
        gate = jnp.where(first, table[:, 2:3], 0.0) + jnp.where(second, table[:, 3:4], 0.0)
        wide = jnp.broadcast_to(named, (tokens, slots))
        before = jnp.dot(lower, wide.astype(jnp.bfloat16), preferred_element_type=jnp.float32)
        place = before + (owner * CAP).astype(jnp.float32)
        onehot = jnp.where(place == lane, wide, 0.0).astype(jnp.bfloat16)
        picked = jnp.dot(onehot, rows[...], preferred_element_type=jnp.float32)
        out[0, half * tokens : (half + 1) * tokens, :] = (gate * picked).astype(out.dtype)


def place_rows(index, meta, hidden, start, stop):
    tokens = meta.shape[2]
    units = hidden.shape[1]
    count = stop - start
    return pl.pallas_call(
        place_kernel,
        grid_spec=pltpu.PrefetchScalarGridSpec(
            num_scalar_prefetch=1,
            grid=(count,),
            in_specs=[
                pl.BlockSpec((2, 8, tokens), lambda i, ix: (ix[start + i], 0, 0)),
                pl.BlockSpec((2 * CAP, units), lambda i, ix: (ix[18 + start + i], 0)),
            ],
            out_specs=pl.BlockSpec((1, 2 * tokens, units), lambda i, ix: (i, 0, 0)),
        ),
        out_shape=jax.ShapeDtypeStruct((count, 2 * tokens, units), jnp.bfloat16),
        cost_estimate=pl.CostEstimate(
            flops=2 * count * 256 * 240 * (units + 128), bytes_accessed=count * 512 * units * 2, transcendentals=0
        ),
        compiler_params=pltpu.CompilerParams(vmem_limit_bytes=VMEM_BYTES),
        name="place_rows",
    )(index, meta, hidden)


def block_dots(index, start, rows, hidden, weight, dots):
    for b, part in enumerate(rows):
        output = jnp.dot(hidden[b], weight[...], preferred_element_type=jnp.float32)
        column = jnp.sum(part[...].astype(jnp.float32) * output, axis=1, keepdims=True)
        line = jnp.transpose(jnp.broadcast_to(column, (column.shape[0], 128)))[0:1]
        for half in range(2):
            owner = index[34 + 2 * (start + b) + half]
            dots[pl.ds(owner, 1)] = line[:, half * 128 : (half + 1) * 128].reshape(1, 1, 128)


def add_grads(rows, hidden, before, after):
    total = None if before is None else before[...]
    for b, part in enumerate(rows):
        term = lax.dot_general(
            hidden[b], part[...], (((0,), (0,)), ((), ())), preferred_element_type=jnp.float32
        )
        total = term if total is None else total + term
    after[...] = total.astype(after.dtype)


def round_call(index, start, rows, placed, weight, grads, dots):
    count = len(rows)
    units, width = weight.shape
    tokens = rows[0].shape[0]
    first = grads is None

    def kernel(ix, hid, wgt, *refs):
        parts, refs = refs[:count], refs[count:]
        if first:
            grads_out, dots_out = refs
            dots_out[...] = jnp.zeros_like(dots_out)
            grads_in = None
        else:
            grads_in, dots_in, grads_out, dots_out = refs
            dots_out[...] = dots_in[...]
        block_dots(ix, start, parts, hid, wgt, dots_out)
        add_grads(parts, hid, grads_in, grads_out)

    whole = lambda shape: pl.BlockSpec(shape, lambda i, ix: (0,) * len(shape))
    hid_spec = pl.BlockSpec((count, tokens, units), lambda i, ix: (0, 0, 0))
    in_specs = [hid_spec, whole(weight.shape)] + [whole(rows[0].shape)] * count
    operands = [placed, weight, *rows]
    aliases = {}
    if not first:
        in_specs += [whole((units, width)), whole((32, 1, 128))]
        operands += [grads, dots]
        aliases = {count + 3: 0, count + 4: 1}
    return pl.pallas_call(
        kernel,
        grid_spec=pltpu.PrefetchScalarGridSpec(
            num_scalar_prefetch=1,
            grid=(1,),
            in_specs=in_specs,
            out_specs=[whole((units, width)), whole((32, 1, 128))],
        ),
        out_shape=[
            jax.ShapeDtypeStruct((units, width), jnp.float32),
            jax.ShapeDtypeStruct((32, 1, 128), jnp.float32),
        ],
        input_output_aliases=aliases,
        cost_estimate=pl.CostEstimate(
            flops=4 * count * tokens * units * width,
            bytes_accessed=8 * units * width + count * tokens * (units + width) * 2,
            transcendentals=0,
        ),
        compiler_params=pltpu.CompilerParams(vmem_limit_bytes=VMEM_BYTES),
        name="round_blocks",
    )(index, *operands)


def last_dots(index, start, rows, placed, weight, dots):
    count = len(rows)
    tokens = rows[0].shape[0]

    def kernel(ix, hid, wgt, *refs):
        parts, (dots_in, dots_out) = refs[:count], refs[count:]
        dots_out[...] = dots_in[...]
        block_dots(ix, start, parts, hid, wgt, dots_out)

    whole = lambda shape: pl.BlockSpec(shape, lambda i, ix: (0,) * len(shape))
    return pl.pallas_call(
        kernel,
        grid_spec=pltpu.PrefetchScalarGridSpec(
            num_scalar_prefetch=1,
            grid=(1,),
            in_specs=[whole(placed.shape), whole(weight.shape)]
            + [whole(rows[0].shape)] * count
            + [whole((32, 1, 128))],
            out_specs=whole((32, 1, 128)),
        ),
        out_shape=jax.ShapeDtypeStruct((32, 1, 128), jnp.float32),
        input_output_aliases={count + 3: 0},
        cost_estimate=pl.CostEstimate(
            flops=2 * count * tokens * weight.size, bytes_accessed=2 * weight.size, transcendentals=0
        ),
        compiler_params=pltpu.CompilerParams(vmem_limit_bytes=VMEM_BYTES),
        name="last_dots",
    )(index, *([placed, weight, *rows, dots]))


def last_grads(which, rows, placed, grads):
    count = len(rows)
    tokens = rows[0].shape[0]
    units, width = grads.shape
    half = units // 2

    def kernel(ix, hid, grads_in, *refs):
        parts, (out,) = refs[:count], refs[count:]
        add_grads(parts, hid, grads_in, out)

    whole = lambda shape: pl.BlockSpec(shape, lambda i, ix: (0,) * len(shape))
    return pl.pallas_call(
        kernel,
        grid_spec=pltpu.PrefetchScalarGridSpec(
            num_scalar_prefetch=1,
            grid=(1,),
            in_specs=[
                pl.BlockSpec((count, tokens, half), lambda i, ix: (0, 0, ix[0])),
                pl.BlockSpec((half, width), lambda i, ix: (ix[0], 0)),
            ]
            + [whole(rows[0].shape)] * count,
            out_specs=whole((half, width)),
        ),
        out_shape=jax.ShapeDtypeStruct((half, width), jnp.bfloat16),
        cost_estimate=pl.CostEstimate(
            flops=2 * count * tokens * half * width, bytes_accessed=6 * half * width, transcendentals=0
        ),
        compiler_params=pltpu.CompilerParams(vmem_limit_bytes=VMEM_BYTES),
        name="last_grads",
    )(which, placed, grads, *rows)


def adam_kernel(which, kept, received, weight, first, second, weight_out, first_out, second_out):
    summed = kept[...].astype(jnp.float32) + received[...].astype(jnp.float32)
    held = weight[...].astype(jnp.float32)
    first_new = beta_first * first[...].astype(jnp.float32) + (1.0 - beta_first) * summed
    second_new = (
        beta_second * second[...].astype(jnp.float32) + (1.0 - beta_second) * summed * summed
    )
    first_hat = first_new * (1.0 / (1.0 - beta_first**step_count))
    second_hat = second_new * (1.0 / (1.0 - beta_second**step_count))
    updated = held - learn_rate * (
        first_hat / (jnp.sqrt(second_hat) + epsilon) + decay_rate * held
    )
    weight_out[...] = updated.astype(weight_out.dtype)
    first_out[...] = first_new.astype(first_out.dtype)
    second_out[...] = second_new.astype(second_out.dtype)


def adam_step(which, kept, received, weight, first, second):
    rows, width = kept.shape
    steps = 4
    tile = pl.BlockSpec((rows // steps, width), lambda i, ix: (i, 0))
    return pl.pallas_call(
        adam_kernel,
        grid_spec=pltpu.PrefetchScalarGridSpec(
            num_scalar_prefetch=1,
            grid=(steps,),
            in_specs=[
                tile,
                tile,
                pl.BlockSpec((rows // steps, width), lambda i, ix: (ix[0] * steps + i, 0)),
                tile,
                tile,
            ],
            out_specs=[tile] * 3,
        ),
        out_shape=[jax.ShapeDtypeStruct(kept.shape, jnp.bfloat16)] * 3,
        cost_estimate=pl.CostEstimate(
            flops=30 * rows * width, bytes_accessed=16 * rows * width, transcendentals=2 * rows * width
        ),
        compiler_params=pltpu.CompilerParams(vmem_limit_bytes=VMEM_BYTES),
        name="adam_step",
    )(which, kept, received, weight, first, second)


def shards(upstream, routes, gates, hidden_saved, down_weight, first_moment, second_moment):
    rows_in = upstream[0]
    route_dev = routes[0]
    gate_dev = gates[0]
    weight = down_weight[0, 0]
    tokens, row_width = rows_in.shape
    units, part = weight.shape
    position = lax.axis_index("ep")
    chip, core = position // 2, position % 2
    parity = chip % 2
    expert, block = position // 8, position % 4

    source = (chip + jnp.array(OFFSETS, jnp.int32)) % 16
    hidden_at = ((source // 4) ^ block) * 4 + source % 4
    owners = (2 * source[:, None] + (core ^ jnp.arange(2, dtype=jnp.int32))[None, :]).reshape(-1)
    index = jnp.concatenate([source, jnp.stack([expert, core]), hidden_at, owners]).astype(jnp.int32)

    def features(at):
        return lax.dynamic_slice(rows_in, (0, at * part), (tokens, part))

    tie = lax.optimization_barrier
    own_hidden = hidden_saved[0, 0]
    chip_hidden = swap_bits(own_hidden, 2)
    outgoing = jnp.stack([features(block ^ 1), features(block ^ 3)])
    incoming = swap_bits(outgoing, 1)
    core_hidden = swap_bits(own_hidden, 1)
    same = jnp.concatenate([features(block), incoming[0]], axis=0)
    diff = jnp.concatenate([features(block ^ 2), incoming[1]], axis=0)
    meta = jnp.concatenate([route_dev.astype(jnp.float32), gate_dev], axis=1)
    meta = jnp.pad(meta.T, ((0, 4), (0, 0)))
    meta = jnp.broadcast_to(meta[None], (lax.axis_size("ep"),) + meta.shape)
    meta = lax.all_to_all(meta, "ep", split_axis=0, concat_axis=0, tiled=True)
    same, diff, chip_hidden, core_hidden = tie((same, diff, chip_hidden, core_hidden))

    def step(pair, hops, *done):
        pair = tie((*pair, *done)) if done else pair
        return send_chips(pair[0], hops), send_chips(pair[1], -hops)

    def round_at(number, rows, grads, dots):
        start, stop = ROUNDS[number]
        return round_call(index, start, rows, placed[start:stop], weight, grads, dots)

    d1 = step((diff, diff), 1)
    s1 = step((same, same), 2)
    far_hidden = swap_bits(chip_hidden, 1)
    hidden = jnp.concatenate([own_hidden, core_hidden, chip_hidden, far_hidden], axis=0)
    d2 = step(d1, 2)
    s2 = step(s1, 2, meta)
    placed = place_rows(index, meta, hidden, 0, 16)
    d3 = step(d2, 2, placed)
    grads, dots = round_at(0, [same, *d1, *s1], None, None)
    s3 = step(s2, 2)
    d4 = step(d3, 2)
    grads1, dots = round_at(1, [*d2, *s2], grads, dots)
    ahead = s3
    across = (send_chips(ahead[0][:tokens], 2), send_chips(ahead[1][tokens:], -2))
    grads, dots = round_at(2, [*d3, *s3], grads1, dots)
    start, stop = ROUNDS[3]
    last = [*d4, jnp.concatenate(across, axis=0)]
    placed_last = placed[start:stop]

    pipe_rank = lax.axis_index("pp")
    rank_count = lax.axis_size("pp")
    upper = (pipe_rank >= rank_count // 2).astype(jnp.int32)
    half_units = units // 2
    moving = last_grads(jnp.stack([1 - upper]), last, placed_last, grads)
    received = lax.ppermute(moving, "pp", [(i, rank_count - 1 - i) for i in range(rank_count)])
    dots = last_dots(index, start, last, placed_last, weight, tie((dots, moving))[0])
    returned = lax.all_to_all(dots, "ep", split_axis=0, concat_axis=0, tiled=True)
    kept = last_grads(jnp.stack([upper]), last, placed_last, grads)

    new_weight, first_new, second_new = adam_step(
        jnp.stack([upper]), kept, received, weight, first_moment[0, 0], second_moment[0, 0]
    )

    returned = tie((returned, new_weight))[0]
    totals = jnp.sum(returned.reshape(EXP, 8, tokens), axis=1)
    named = route_dev[:, :, None] == jnp.arange(EXP, dtype=jnp.int32)[None, None, :]
    gate_grad = jnp.sum(jnp.where(named, totals.T[:, None, :], 0.0), axis=2) / gate_dev
    return (
        gate_grad[None],
        new_weight[None, None],
        first_new[None, None],
        second_new[None, None],
    )


def solution(mesh):
    placed = (
        P("pp", "ep", None),
        P("pp", "ep", None),
        P("pp", "ep", None),
        P("pp", "ep", None, None),
        P("pp", "ep", None, None),
        P("pp", "ep", None, None),
        P("pp", "ep", None, None),
    )
    return jax.shard_map(
        shards,
        mesh=mesh,
        in_specs=placed,
        out_specs=(
            P("pp", "ep", None),
            P("pp", "ep", None, None),
            P("pp", "ep", None, None),
            P("pp", "ep", None, None),
        ),
        check_vma=False,
    )
```

```python
import jax
import jax.numpy as jnp
from jax import lax
from jax.experimental import pallas as pl
from jax.experimental.pallas import tpu as pltpu
from jax.sharding import PartitionSpec as P

EXP = 4
TOP = 2
SPLITS = 2
CAP = 120

beta_first = 0.9
beta_second = 0.95
learn_rate = 0.00022
decay_rate = 0.1
epsilon = 1e-08
step_count = 10

VMEM_BYTES = 40 * 1024 * 1024

OFFSETS = (0, -1, 1, -2, 2, -3, 3, -4, 4, -5, 5, -6, 6, -7, 7, 8)
ROUNDS = ((0, 5), (5, 9), (9, 13), (13, 16))


def send_chips(block, hops):
    count = lax.axis_size("ep")
    return lax.ppermute(block, "ep", [(i, (i + 2 * hops) % count) for i in range(count)])


def swap_bits(block, bits):
    count = lax.axis_size("ep")
    return lax.ppermute(block, "ep", [(i, i ^ bits) for i in range(count)])


def place_kernel(index, *refs):
    count = (len(refs) - 1) // 2
    metas, parts, out = refs[:count], refs[count : 2 * count], refs[-1]
    expert, core = index[16], index[17]
    tokens = metas[0].shape[2]
    slots = parts[0].shape[0]
    lower = lax.broadcasted_iota(jnp.int32, (tokens, tokens), 0) > lax.broadcasted_iota(
        jnp.int32, (tokens, tokens), 1
    )
    lower = lower.astype(jnp.float32).astype(jnp.bfloat16)
    lane = lax.broadcasted_iota(jnp.int32, (tokens, slots), 1).astype(jnp.float32)
    wanted = expert.astype(jnp.float32)
    for chip in range(count):
        for half in range(2):
            owner = core if half == 0 else 1 - core
            table = jnp.transpose(metas[chip][owner])
            first = table[:, 0:1] == wanted
            second = table[:, 1:2] == wanted
            named = jnp.where(first | second, 1.0, 0.0)
            gate = jnp.where(first, table[:, 2:3], 0.0) + jnp.where(second, table[:, 3:4], 0.0)
            wide = jnp.broadcast_to(named, (tokens, slots))
            before = jnp.dot(lower, wide.astype(jnp.bfloat16), preferred_element_type=jnp.float32)
            place = before + (owner * CAP).astype(jnp.float32)
            onehot = jnp.where(place == lane, wide, 0.0).astype(jnp.bfloat16)
            picked = jnp.dot(onehot, parts[chip][...], preferred_element_type=jnp.float32)
            out[chip, half * tokens : (half + 1) * tokens, :] = (gate * picked).astype(out.dtype)


def place_rows(index, meta, hidden):
    tokens = meta.shape[2]
    units = hidden.shape[1]
    chips = 4

    def meta_spec(k):
        return pl.BlockSpec((2, 8, tokens), lambda i, ix: (ix[chips * i + k], 0, 0))

    def part_spec(k):
        return pl.BlockSpec((2 * CAP, units), lambda i, ix: (ix[18 + chips * i + k], 0))

    return pl.pallas_call(
        place_kernel,
        grid_spec=pltpu.PrefetchScalarGridSpec(
            num_scalar_prefetch=1,
            grid=(16 // chips,),
            in_specs=[meta_spec(k) for k in range(chips)] + [part_spec(k) for k in range(chips)],
            out_specs=pl.BlockSpec((chips, 2 * tokens, units), lambda i, ix: (i, 0, 0)),
        ),
        out_shape=jax.ShapeDtypeStruct((16, 2 * tokens, units), jnp.bfloat16),
        cost_estimate=pl.CostEstimate(
            flops=2 * 16 * 256 * 240 * (units + 128), bytes_accessed=16 * 512 * units * 2, transcendentals=0
        ),
        compiler_params=pltpu.CompilerParams(vmem_limit_bytes=VMEM_BYTES),
        name="place_rows",
    )(index, *([meta] * chips), *([hidden] * chips))


def block_dots(index, start, rows, hidden, weight, dots):
    for b, part in enumerate(rows):
        output = jnp.dot(hidden[b], weight[...], preferred_element_type=jnp.float32)
        column = jnp.sum(part[...].astype(jnp.float32) * output, axis=1, keepdims=True)
        line = jnp.transpose(jnp.broadcast_to(column, (column.shape[0], 128)))[0:1]
        for half in range(2):
            owner = index[34 + 2 * (start + b) + half]
            dots[pl.ds(owner, 1)] = line[:, half * 128 : (half + 1) * 128].reshape(1, 1, 128)


def add_grads(rows, hidden, before, after):
    total = None if before is None else before[...]
    for b, part in enumerate(rows):
        term = lax.dot_general(
            hidden[b], part[...], (((0,), (0,)), ((), ())), preferred_element_type=jnp.float32
        )
        total = term if total is None else total + term
    after[...] = total.astype(after.dtype)


def round_call(index, start, rows, placed, weight, grads, dots):
    count = len(rows)
    units, width = weight.shape
    tokens = rows[0].shape[0]
    first = grads is None

    def kernel(ix, hid, wgt, *refs):
        parts, refs = refs[:count], refs[count:]
        if first:
            grads_out, dots_out = refs
            dots_out[...] = jnp.zeros_like(dots_out)
            grads_in = None
        else:
            grads_in, dots_in, grads_out, dots_out = refs
            dots_out[...] = dots_in[...]
        block_dots(ix, start, parts, hid, wgt, dots_out)
        add_grads(parts, hid, grads_in, grads_out)

    whole = lambda shape: pl.BlockSpec(shape, lambda i, ix: (0,) * len(shape))
    hid_spec = pl.BlockSpec((count, tokens, units), lambda i, ix: (0, 0, 0))
    in_specs = [hid_spec, whole(weight.shape)] + [whole(rows[0].shape)] * count
    operands = [placed, weight, *rows]
    aliases = {}
    if not first:
        in_specs += [whole((units, width)), whole((32, 1, 128))]
        operands += [grads, dots]
        aliases = {count + 3: 0, count + 4: 1}
    return pl.pallas_call(
        kernel,
        grid_spec=pltpu.PrefetchScalarGridSpec(
            num_scalar_prefetch=1,
            grid=(1,),
            in_specs=in_specs,
            out_specs=[whole((units, width)), whole((32, 1, 128))],
        ),
        out_shape=[
            jax.ShapeDtypeStruct((units, width), jnp.float32),
            jax.ShapeDtypeStruct((32, 1, 128), jnp.float32),
        ],
        input_output_aliases=aliases,
        cost_estimate=pl.CostEstimate(
            flops=4 * count * tokens * units * width,
            bytes_accessed=8 * units * width + count * tokens * (units + width) * 2,
            transcendentals=0,
        ),
        compiler_params=pltpu.CompilerParams(vmem_limit_bytes=VMEM_BYTES),
        name="round_blocks",
    )(index, *operands)


def last_dots(index, start, rows, placed, weight, dots):
    count = len(rows)
    tokens = rows[0].shape[0]

    def kernel(ix, hid, wgt, *refs):
        parts, (dots_in, dots_out) = refs[:count], refs[count:]
        dots_out[...] = dots_in[...]
        block_dots(ix, start, parts, hid, wgt, dots_out)

    whole = lambda shape: pl.BlockSpec(shape, lambda i, ix: (0,) * len(shape))
    return pl.pallas_call(
        kernel,
        grid_spec=pltpu.PrefetchScalarGridSpec(
            num_scalar_prefetch=1,
            grid=(1,),
            in_specs=[whole(placed.shape), whole(weight.shape)]
            + [whole(rows[0].shape)] * count
            + [whole((32, 1, 128))],
            out_specs=whole((32, 1, 128)),
        ),
        out_shape=jax.ShapeDtypeStruct((32, 1, 128), jnp.float32),
        input_output_aliases={count + 3: 0},
        cost_estimate=pl.CostEstimate(
            flops=2 * count * tokens * weight.size, bytes_accessed=2 * weight.size, transcendentals=0
        ),
        compiler_params=pltpu.CompilerParams(vmem_limit_bytes=VMEM_BYTES),
        name="last_dots",
    )(index, *([placed, weight, *rows, dots]))


def last_grads(which, rows, placed, grads):
    count = len(rows)
    tokens = rows[0].shape[0]
    units, width = grads.shape
    half = units // 2

    def kernel(ix, hid, grads_in, *refs):
        parts, (out,) = refs[:count], refs[count:]
        add_grads(parts, hid, grads_in, out)

    whole = lambda shape: pl.BlockSpec(shape, lambda i, ix: (0,) * len(shape))
    return pl.pallas_call(
        kernel,
        grid_spec=pltpu.PrefetchScalarGridSpec(
            num_scalar_prefetch=1,
            grid=(1,),
            in_specs=[
                pl.BlockSpec((count, tokens, half), lambda i, ix: (0, 0, ix[0])),
                pl.BlockSpec((half, width), lambda i, ix: (ix[0], 0)),
            ]
            + [whole(rows[0].shape)] * count,
            out_specs=whole((half, width)),
        ),
        out_shape=jax.ShapeDtypeStruct((half, width), jnp.bfloat16),
        cost_estimate=pl.CostEstimate(
            flops=2 * count * tokens * half * width, bytes_accessed=6 * half * width, transcendentals=0
        ),
        compiler_params=pltpu.CompilerParams(vmem_limit_bytes=VMEM_BYTES),
        name="last_grads",
    )(which, placed, grads, *rows)


def adam_kernel(which, kept, received, weight, first, second, weight_out, first_out, second_out):
    summed = kept[...].astype(jnp.float32) + received[...].astype(jnp.float32)
    held = weight[...].astype(jnp.float32)
    first_new = beta_first * first[...].astype(jnp.float32) + (1.0 - beta_first) * summed
    second_new = (
        beta_second * second[...].astype(jnp.float32) + (1.0 - beta_second) * summed * summed
    )
    first_hat = first_new * (1.0 / (1.0 - beta_first**step_count))
    second_hat = second_new * (1.0 / (1.0 - beta_second**step_count))
    updated = held - learn_rate * (
        first_hat / (jnp.sqrt(second_hat) + epsilon) + decay_rate * held
    )
    weight_out[...] = updated.astype(weight_out.dtype)
    first_out[...] = first_new.astype(first_out.dtype)
    second_out[...] = second_new.astype(second_out.dtype)


def adam_step(which, kept, received, weight, first, second):
    rows, width = kept.shape
    steps = 4
    tile = pl.BlockSpec((rows // steps, width), lambda i, ix: (i, 0))
    return pl.pallas_call(
        adam_kernel,
        grid_spec=pltpu.PrefetchScalarGridSpec(
            num_scalar_prefetch=1,
            grid=(steps,),
            in_specs=[
                tile,
                tile,
                pl.BlockSpec((rows // steps, width), lambda i, ix: (ix[0] * steps + i, 0)),
                tile,
                tile,
            ],
            out_specs=[tile] * 3,
        ),
        out_shape=[jax.ShapeDtypeStruct(kept.shape, jnp.bfloat16)] * 3,
        cost_estimate=pl.CostEstimate(
            flops=30 * rows * width, bytes_accessed=16 * rows * width, transcendentals=2 * rows * width
        ),
        compiler_params=pltpu.CompilerParams(vmem_limit_bytes=VMEM_BYTES),
        name="adam_step",
    )(which, kept, received, weight, first, second)


def shards(upstream, routes, gates, hidden_saved, down_weight, first_moment, second_moment):
    rows_in = upstream[0]
    route_dev = routes[0]
    gate_dev = gates[0]
    weight = down_weight[0, 0]
    tokens, row_width = rows_in.shape
    units, part = weight.shape
    position = lax.axis_index("ep")
    chip, core = position // 2, position % 2
    parity = chip % 2
    expert, block = position // 8, position % 4

    source = (chip + jnp.array(OFFSETS, jnp.int32)) % 16
    hidden_at = ((source // 4) ^ block) * 4 + source % 4
    owners = (2 * source[:, None] + (core ^ jnp.arange(2, dtype=jnp.int32))[None, :]).reshape(-1)
    index = jnp.concatenate([source, jnp.stack([expert, core]), hidden_at, owners]).astype(jnp.int32)

    def features(at):
        return lax.dynamic_slice(rows_in, (0, at * part), (tokens, part))

    tie = lax.optimization_barrier
    own_hidden = hidden_saved[0, 0]
    chip_hidden = swap_bits(own_hidden, 2)
    outgoing = jnp.stack([features(block ^ 1), features(block ^ 3)])
    incoming = swap_bits(outgoing, 1)
    core_hidden = swap_bits(own_hidden, 1)
    same = jnp.concatenate([features(block), incoming[0]], axis=0)
    diff = jnp.concatenate([features(block ^ 2), incoming[1]], axis=0)
    meta = jnp.concatenate([route_dev.astype(jnp.float32), gate_dev], axis=1)
    meta = jnp.pad(meta.T, ((0, 4), (0, 0)))
    meta = jnp.broadcast_to(meta[None], (lax.axis_size("ep"),) + meta.shape)
    meta = lax.all_to_all(meta, "ep", split_axis=0, concat_axis=0, tiled=True)
    same, diff, chip_hidden, core_hidden = tie((same, diff, chip_hidden, core_hidden))

    def step(pair, hops, *done):
        pair = tie((*pair, *done)) if done else pair
        return send_chips(pair[0], hops), send_chips(pair[1], -hops)

    def round_at(number, rows, grads, dots):
        start, stop = ROUNDS[number]
        return round_call(index, start, rows, placed[start:stop], weight, grads, dots)

    d1 = step((diff, diff), 1)
    s1 = step((same, same), 2)
    far_hidden = swap_bits(chip_hidden, 1)
    hidden = jnp.concatenate([own_hidden, core_hidden, chip_hidden, far_hidden], axis=0)
    d2 = step(d1, 2)
    s2 = step(s1, 2, meta)
    placed = place_rows(index, meta, hidden)
    d3 = step(d2, 2, placed)
    grads, dots = round_at(0, [same, *d1, *s1], None, None)
    s3 = step(s2, 2)
    d4 = step(d3, 2)
    grads1, dots = round_at(1, [*d2, *s2], grads, dots)
    ahead = s3
    across = (send_chips(ahead[0][:tokens], 2), send_chips(ahead[1][tokens:], -2))
    grads, dots = round_at(2, [*d3, *s3], grads1, dots)
    start, stop = ROUNDS[3]
    last = [*d4, jnp.concatenate(across, axis=0)]
    placed_last = placed[start:stop]

    pipe_rank = lax.axis_index("pp")
    rank_count = lax.axis_size("pp")
    upper = (pipe_rank >= rank_count // 2).astype(jnp.int32)
    half_units = units // 2
    moving = last_grads(jnp.stack([1 - upper]), last, placed_last, grads)
    received = lax.ppermute(moving, "pp", [(i, rank_count - 1 - i) for i in range(rank_count)])
    dots = last_dots(index, start, last, placed_last, weight, tie((dots, moving))[0])
    returned = lax.all_to_all(dots, "ep", split_axis=0, concat_axis=0, tiled=True)
    kept = last_grads(jnp.stack([upper]), last, placed_last, grads)

    new_weight, first_new, second_new = adam_step(
        jnp.stack([upper]), kept, received, weight, first_moment[0, 0], second_moment[0, 0]
    )

    returned = tie((returned, new_weight))[0]
    totals = jnp.sum(returned.reshape(EXP, 8, tokens), axis=1)
    named = route_dev[:, :, None] == jnp.arange(EXP, dtype=jnp.int32)[None, None, :]
    gate_grad = jnp.sum(jnp.where(named, totals.T[:, None, :], 0.0), axis=2) / gate_dev
    return (
        gate_grad[None],
        new_weight[None, None],
        first_new[None, None],
        second_new[None, None],
    )


def solution(mesh):
    placed = (
        P("pp", "ep", None),
        P("pp", "ep", None),
        P("pp", "ep", None),
        P("pp", "ep", None, None),
        P("pp", "ep", None, None),
        P("pp", "ep", None, None),
        P("pp", "ep", None, None),
    )
    return jax.shard_map(
        shards,
        mesh=mesh,
        in_specs=placed,
        out_specs=(
            P("pp", "ep", None),
            P("pp", "ep", None, None),
            P("pp", "ep", None, None),
            P("pp", "ep", None, None),
        ),
        check_vma=False,
    )
```
